128 devices in a mesh: wide: 32 (over z, y, x_hi), narrow: 4 (over x_lo, core).
Axes of the slice: x: 4 (x_hi: 2, x_lo: 2; x = x_hi * 2 + x_lo), y: 4, z: 4, core: 2. Of those that a mesh axis runs over, the one named last changes fastest.
Arguments:
- amplitudes: bfloat16 [4, 32768, 4096], P('narrow', None, 'wide'), may hold values from -6 to 6
- integrals: bfloat16 [4, 4096, 512], P('narrow'), may hold values from -0.09375 to 0.09375
- panel_order: int32 [4], replicated, may hold values from 0 to 3, each once
- row_label: int32 [4, 256], P('narrow', 'wide'), may hold values from 0 to 7
- col_label: int32 [32], replicated, may hold values from 0 to 7
- sym_map: int32 [8, 8], replicated, may hold values from 0 to 1
- row_energy: float32 [4, 32768], P('narrow', 'wide'), may hold values from 0.5 to 4
- col_energy: float32 [4, 512], replicated, may hold values from 0.5 to 4
Outputs:
- update: bfloat16 [4, 32768, 2048], P('narrow', 'wide')
The draws below stay inside these ranges and needn't reach their ends.
Inputs may be any that keep to these rules, and one draw needn't show every extreme that they name: `panel_order`: each panel appears once.
All inputs are finite; a program needn't handle non-finite values.
Results may differ from the reference program's by a relative error of at most 0.001.
Values may be sent and summed in bfloat16 or wider, within the bound.
No kernel may reach another device: no remote copies, remote signals or barrier semaphores. Data moves between devices by JAX's collectives and lax.ppermute only.
A program may use at most 192 MiB of HBM per device.

```python
import math
import jax
import jax.numpy as jnp
from jax import lax

BLOCK = 128
LABELS = 8
CONTR = 4096
QP = 512
NPAN = 4
GROUPS = 4
PN = 32768


def set_ends(drawn, rng, low, top_value):
    place = [jax.random.randint(jax.random.fold_in(rng, axis), (), 0, length) for axis, length in enumerate(drawn.shape)]
    main_axis = drawn.shape.index(max(drawn.shape))
    neighbour = place[:main_axis] + [(place[main_axis] + 1) % drawn.shape[main_axis]] + place[main_axis + 1:]
    return drawn.at[tuple(place)].set(low).at[tuple(neighbour)].set(top_value)


def level_of(own_key, dims, cuts, low, top_value):
    def one(axis_at, shards_of):
        heights = jax.random.uniform(jax.random.fold_in(jax.random.fold_in(own_key, 6), axis_at), (shards_of,), jnp.float32, low / len(cuts), top_value / len(cuts))
        return jnp.repeat(jnp.exp(heights), dims[axis_at] // shards_of).reshape((-1,) + (1,) * (len(dims) - axis_at - 1))

    level = one(*cuts[0])
    for cut in cuts[1:]:
        level = level * one(*cut)
    return level


def scatter_about(rng, dims, scale, bound, shards=(), kind=jnp.bfloat16):
    entries = jax.random.normal(rng, dims, jnp.float32) * scale
    if len(shards) > 0:
        entries = level_of(rng, dims, shards, -0.22, 0.18) * entries
    return jnp.clip(entries, min=-bound, max=bound).astype(kind)


def setup_inputs(seed: int = 0) -> dict:
    keys = jax.random.split(jax.random.key(seed), 9)
    return {
        "amplitudes": scatter_about(keys[0], (GROUPS, PN, CONTR), 1.0, 6.0, ((0, 4), (2, 32))),
        "integrals": scatter_about(keys[1], (NPAN, CONTR, QP), CONTR ** -0.5, 0.09375, ((0, 4),)),
        "panel_order": jax.random.permutation(keys[2], NPAN).astype(jnp.int32),
        "row_label": set_ends(jax.random.randint(keys[3], (GROUPS, PN // BLOCK), 0, LABELS), jax.random.fold_in(keys[3], 1), 0, LABELS - 1).astype(jnp.int32),
        "col_label": set_ends(jax.random.randint(keys[4], (CONTR // BLOCK,), 0, LABELS), jax.random.fold_in(keys[4], 1), 0, LABELS - 1).astype(jnp.int32),
        "sym_map": set_ends(jax.random.randint(keys[5], (LABELS, LABELS), 0, 2), jax.random.fold_in(keys[5], 1), 0, 1).astype(jnp.int32),
        "row_energy": jnp.clip(jnp.exp(math.log(4.0) - 2.0794415 * jax.random.uniform(keys[6], (GROUPS, PN), jnp.float32) ** level_of(keys[6], (GROUPS, PN), ((0, 4), (1, 32)), -0.2, 0.2)), 0.5, 4.0),
        "col_energy": jnp.clip(jnp.exp(jax.random.uniform(keys[7], (NPAN, QP), jnp.float32, math.log(0.5), math.log(4.0))), 0.5, 4.0),
    }


def block_mask(labels_row, labels_col, sym_map):
    table = sym_map.astype(jnp.float32)
    left = (labels_row[:, None] == jnp.arange(LABELS, dtype=jnp.int32)[None, :]).astype(jnp.float32)
    right = (labels_col[:, None] == jnp.arange(LABELS, dtype=jnp.int32)[None, :]).astype(jnp.float32)
    return jnp.dot(jnp.dot(left, table), right.T)


def one_group(amplitudes_g, row_label_g, row_energy_g, col_label, sym_map, integrals, panel_order, col_energy):
    mask = block_mask(row_label_g, col_label, sym_map).astype(jnp.bfloat16)
    rows = amplitudes_g.shape[0]
    nbr = rows // BLOCK
    nbc = CONTR // BLOCK
    masked = (amplitudes_g.reshape(nbr, BLOCK, nbc, BLOCK) * mask[:, None, :, None]).reshape(rows, CONTR)
    pieces = []
    for slot in range(NPAN):
        index = panel_order[slot]
        panel = lax.dynamic_index_in_dim(integrals, index, 0, keepdims=False)
        energy = lax.dynamic_index_in_dim(col_energy, index, 0, keepdims=False)
        cycle = jnp.dot(masked, panel, preferred_element_type=jnp.float32)
        pieces.append(cycle / (row_energy_g[:, None] + energy[None, :]))
    return jnp.concatenate(pieces, axis=1).astype(jnp.bfloat16)


def reference(amplitudes, integrals, panel_order, row_label, col_label, sym_map, row_energy, col_energy):
    def step(items):
        return one_group(items[0], items[1], items[2], col_label, sym_map, integrals, panel_order, col_energy)
    return lax.map(step, (amplitudes, row_label, row_energy))
```

```python
import functools
import jax
import jax.numpy as jnp
from jax import lax
from jax.experimental import pallas as pl
from jax.experimental.pallas import tpu as pltpu
from jax.sharding import PartitionSpec as P

AXES = ("wide", "narrow")
CHUNKS = (512, 512)


def x_of(device):
    return device // 4 % 2 * 2 + device // 2 % 2


def shift_x(devices, step):
    pairs = []
    for i in range(devices):
        x = (x_of(i) + step) % 4
        pairs.append((i, i // 8 * 8 + x // 2 * 4 + x % 2 * 2 + i % 2))
    return pairs


def swap_core(devices):
    return [(i, i ^ 1) for i in range(devices)]


def cycle_kernel(
    held_ref, slot_ref, row_label_ref, col_label_ref, sym_ref,
    amp_ref, row_energy_ref, col_energy_ref, *refs, first, blk, pieces
):
    panel_refs = refs[: sum(pieces)]
    refs = refs[sum(pieces):]
    if len(refs) == 5:
        refs = refs[1:]
    out_ref, masked, panel, sems = refs
    step = pl.program_id(0)
    nbc = amp_ref.shape[0]
    rows = amp_ref.shape[1]
    depth = panel.shape[1]

    def copies(k):
        at = sum(pieces[:k])
        size = depth // pieces[k]
        return [
            pltpu.make_async_copy(
                panel_refs[at + i], panel.at[k, pl.ds(i * size, size)], sems.at[at + i]
            )
            for i in range(pieces[k])
        ]

    @pl.when(step == 0)
    def _():
        for k in range(len(pieces)):
            for copy in copies(k):
                copy.start()
        for i in range(rows // blk):
            for c in range(nbc):
                keep = sym_ref[row_label_ref[first + i], col_label_ref[c]]
                tile = amp_ref[c, i * blk:(i + 1) * blk, :]
                masked[i * blk:(i + 1) * blk, c * blk:(c + 1) * blk] = tile * keep.astype(
                    jnp.float32
                ).astype(tile.dtype)

    for k in range(len(pieces)):

        @pl.when(step == k)
        def _():
            for copy in copies(k):
                copy.wait()

    cycle = jnp.dot(masked[...], panel[step], preferred_element_type=jnp.float32)
    energy = row_energy_ref[...] + col_energy_ref[pl.ds(held_ref[step], 1), :]
    out_ref[...] = (cycle / energy).astype(out_ref.dtype)


def update_rows(amp, panels, before, start, total, scalars, row_energy, col_energy, blk):
    nbc, rows, _ = amp.shape
    pieces = tuple(len(p) for p in panels)
    flat = [piece for p in panels for piece in p]
    depth = sum(p.shape[0] for p in panels[0])
    qp = flat[0].shape[1]
    at = start // rows
    slots = len(panels)
    whole = pl.BlockSpec(memory_space=pl.ANY)
    in_specs = [
        pl.BlockSpec((nbc, rows, blk), lambda k, *_: (0, 0, 0)),
        pl.BlockSpec((rows, 1), lambda k, *_: (at, 0)),
        pl.BlockSpec(col_energy.shape, lambda k, *_: (0, 0)),
    ] + [whole] * len(flat)
    args = [amp, row_energy, col_energy] + flat
    aliases = {}
    if before is not None:
        in_specs.append(whole)
        args.append(before)
        aliases = {len(scalars) + len(args) - 1: 0}
    return pl.pallas_call(
        functools.partial(cycle_kernel, first=start // blk, blk=blk, pieces=pieces),
        grid_spec=pltpu.PrefetchScalarGridSpec(
            num_scalar_prefetch=len(scalars),
            grid=(slots,),
            in_specs=in_specs,
            out_specs=pl.BlockSpec((rows, qp), lambda k, held, slot, *_: (at, slot[k])),
            scratch_shapes=[
                pltpu.VMEM((rows, depth), amp.dtype),
                pltpu.VMEM((slots, depth, qp), amp.dtype),
                pltpu.SemaphoreType.DMA((len(flat),)),
            ],
        ),
        out_shape=jax.ShapeDtypeStruct((total, slots * qp), jnp.bfloat16),
        input_output_aliases=aliases,
        compiler_params=pltpu.CompilerParams(vmem_limit_bytes=44 * 2**20),
        cost_estimate=pl.CostEstimate(
            flops=2 * rows * depth * qp * slots,
            bytes_accessed=2 * (rows * depth + slots * depth * qp + rows * slots * qp),
            transcendentals=0,
        ),
    )(*scalars, *args)


def per_device(
    amplitudes, integrals, panel_order, row_label, col_label, sym_map, row_energy, col_energy
):
    wide, narrow = lax.axis_size("wide"), lax.axis_size("narrow")
    devices = wide * narrow
    send = functools.partial(lax.ppermute, axis_name=AXES)
    own = integrals[0]
    half = own.shape[0] // 2
    far = [
        send(own[:half], perm=shift_x(devices, 1)),
        send(own[half:], perm=shift_x(devices, -1)),
    ]
    twin = send(own, perm=swap_core(devices))
    far_twin = [send(piece, perm=swap_core(devices)) for piece in far]
    panels = [[own], [twin], far, far_twin]
    me = lax.axis_index("narrow")
    held = jnp.stack([me, me ^ 1, me ^ 2, me ^ 3]).astype(jnp.int32)
    slot = jnp.sum(
        jnp.where(
            held[:, None] == panel_order[None, :],
            jnp.arange(narrow, dtype=jnp.int32)[None, :],
            0,
        ),
        axis=1,
    ).astype(jnp.int32)
    total = amplitudes.shape[1] // wide
    blk = amplitudes.shape[2]
    by_target = amplitudes[0].reshape(wide, total, blk)
    scalars = (held, slot, row_label[0], col_label, sym_map)
    column = row_energy.reshape(total, 1)
    out = None
    start = 0
    for rows in CHUNKS:
        amp = lax.all_to_all(by_target[:, start:start + rows], "wide", split_axis=0, concat_axis=0)
        out = update_rows(
            amp, panels, out, start, total, scalars, column, col_energy, blk
        )
        start += rows
    return out[None]


def solution(mesh):
    in_specs = (
        P("narrow", None, "wide"),
        P("narrow", None, None),
        P(),
        P("narrow", "wide"),
        P(),
        P(),
        P("narrow", "wide"),
        P(),
    )
    out_specs = P("narrow", "wide", None)
    return jax.shard_map(
        per_device, mesh=mesh, in_specs=in_specs, out_specs=out_specs, check_vma=False
    )
```

```python
import functools
import jax
import jax.numpy as jnp
from jax import lax
from jax.experimental import pallas as pl
from jax.experimental.pallas import tpu as pltpu
from jax.sharding import PartitionSpec as P

AXES = ("wide", "narrow")
CHUNKS = (640, 384)
ANY = pl.BlockSpec(memory_space=pl.ANY)
VMEM = pl.BlockSpec(memory_space=pltpu.VMEM)
HBM = pl.BlockSpec(memory_space=pltpu.HBM)
SMEM = pl.BlockSpec(memory_space=pltpu.SMEM)


def place(i):
    return i // 32, i // 8 % 4, i // 4 % 2 * 2 + i // 2 % 2, i % 2


def shift(devices, dz=0, dy=0, dx=0, dc=0):
    pairs = []
    for i in range(devices):
        z, y, x, c = place(i)
        z, y, x, c = (z + dz) % 4, (y + dy) % 4, (x + dx) % 4, (c + dc) % 2
        pairs.append((i, z * 32 + y * 8 + x // 2 * 4 + x % 2 * 2 + c))
    return pairs


def after(value, *others):
    return lax.optimization_barrier((value, *others))[0]


def cycle_kernel(
    scalar_ref, amp_ref, row_energy_ref, col_energy_ref, *refs, start, slots, labels, cuts
):
    *refs, masked, staged, panels, store_sems, load_sems, keep_sems = refs
    out_ref = refs[-2] if cuts else refs[-1]
    kept = refs[-1] if cuts else refs[0]
    count = max((which for which, _, _ in cuts), default=-1) + 1
    nbc, rows, blk = amp_ref.shape
    qp = staged.shape[2]
    held, slot, row_label = 0, slots, 2 * slots
    col_label = row_label + labels[0]
    table = col_label + nbc
    offset = table + labels[1] * labels[1]

    def loads(k):
        if not cuts:
            return [pltpu.make_async_copy(kept.at[k], panels.at[k], load_sems.at[k])]
        if k < 2:
            return [pltpu.make_async_copy(refs[k], panels.at[k], load_sems.at[k])]
        out = []
        for n, (which, at, size) in enumerate(cuts):
            to = pl.multiple_of(scalar_ref[offset + n], 128)
            out.append(
                pltpu.make_async_copy(
                    refs[2 + (k - 2) * count + which].at[pl.ds(at, size)],
                    panels.at[k, pl.ds(to, size)],
                    load_sems.at[k],
                )
            )
        return out

    def mask_column(c, carry):
        for i in range(rows // blk):
            row = scalar_ref[row_label + start // blk + i]
            kept_block = scalar_ref[table + row * labels[1] + scalar_ref[col_label + c]]
            tile = amp_ref[c, i * blk:(i + 1) * blk, :]
            at = pl.multiple_of(c * blk, blk)
            masked[i * blk:(i + 1) * blk, pl.ds(at, blk)] = tile * kept_block.astype(
                jnp.float32
            ).astype(tile.dtype)
        return carry

    def store(k):
        at = pl.multiple_of(scalar_ref[slot + k] * qp, qp)
        return pltpu.make_async_copy(
            staged.at[k], out_ref.at[pl.ds(start, rows), pl.ds(at, qp)], store_sems.at[k]
        )

    def keep(k):
        return pltpu.make_async_copy(panels.at[k], kept.at[k], keep_sems.at[k])

    for copy in loads(0):
        copy.start()
    lax.fori_loop(0, nbc, mask_column, 0)
    for copy in loads(1):
        copy.start()
    for k in range(slots):
        for copy in loads(k):
            copy.wait()
        if k + 2 < slots:
            for copy in loads(k + 2):
                copy.start()
        if cuts:
            keep(k).start()
        cycle = jnp.dot(masked[...], panels[k], preferred_element_type=jnp.float32)
        energy = row_energy_ref[...] + col_energy_ref[pl.ds(scalar_ref[held + k], 1), :]
        staged[k] = (cycle / energy).astype(staged.dtype)
        store(k).start()
    for k in range(slots):
        store(k).wait()
        if cuts:
            keep(k).wait()


def update_rows(amp, panels, cuts, before, start, total, scalars, labels, row_energy, col_energy):
    nbc, rows, blk = amp.shape
    depth, qp = nbc * blk, panels[0].shape[-1]
    slots = 4
    args = [scalars, amp, row_energy[start:start + rows], col_energy] + panels
    specs = [SMEM] + [VMEM] * 3
    out_shape = [jax.ShapeDtypeStruct((total, slots * qp), jnp.bfloat16)]
    aliases = {}
    if before is None:
        specs += [HBM] * len(panels)
        out_shape.append(jax.ShapeDtypeStruct((slots, depth, qp), amp.dtype))
    else:
        specs += [HBM, ANY]
        aliases = {len(args): 0}
        args.append(before)
        cuts = ()
    return pl.pallas_call(
        functools.partial(cycle_kernel, start=start, slots=slots, labels=labels, cuts=cuts),
        in_specs=specs,
        out_specs=[ANY, HBM][: len(out_shape)],
        scratch_shapes=[
            pltpu.VMEM((rows, depth), amp.dtype),
            pltpu.VMEM((slots, rows, qp), jnp.bfloat16),
            pltpu.VMEM((slots, depth, qp), amp.dtype),
            pltpu.SemaphoreType.DMA((slots,)),
            pltpu.SemaphoreType.DMA((slots,)),
            pltpu.SemaphoreType.DMA((slots,)),
        ],
        out_shape=out_shape,
        input_output_aliases=aliases,
        compiler_params=pltpu.CompilerParams(vmem_limit_bytes=(54 if before is None else 50) * 2**20),
        cost_estimate=pl.CostEstimate(
            flops=2 * rows * depth * qp * slots,
            bytes_accessed=2 * (rows * depth + slots * depth * qp + rows * slots * qp),
            transcendentals=0,
        ),
    )(*args)


def per_device(
    amplitudes, integrals, panel_order, row_label, col_label, sym_map, row_energy, col_energy
):
    wide, narrow = lax.axis_size("wide"), lax.axis_size("narrow")
    total = amplitudes.shape[1] // wide
    blk = amplitudes.shape[2]
    by_target = amplitudes[0].reshape(wide, total, blk)

    def send(value, **way):
        return lax.ppermute(value, AXES, shift(wide * narrow, **way))

    own = integrals[0]
    depth = own.shape[0]
    half, part, bit = depth // 2, depth // 8, depth // 16
    w = lax.axis_index("wide")
    z, y = w // 8, w // 2 % 4

    def a_at(step):
        return (z + 2 * y + 4 + step) % 4 * part

    def b_at(step):
        return half + (2 * z + y + 4 + step) % 4 * part

    a = send(lax.dynamic_slice_in_dim(own, a_at(0), part, 0), dx=1)
    b = send(lax.dynamic_slice_in_dim(own, b_at(0), part, 0), dx=-1)
    twin = send(own, dc=1)
    amps, start = [], 0
    for rows in CHUNKS:
        block = by_target[:, start:start + rows]
        gate = amps[-1:] if amps else [a, b, twin]
        block = after(block, *gate)
        amps.append(lax.all_to_all(block, "wide", split_axis=0, concat_axis=0))
        start += rows
    z_down = send(jnp.concatenate([a, b[:bit]]), dz=1)
    z_up = send(jnp.concatenate([a, b[bit:]]), dz=-1)
    y_down = send(jnp.concatenate([b, a[:bit]]), dy=1)
    y_up = send(jnp.concatenate([b, a[bit:]]), dy=-1)
    pieces = [a, b, z_down, z_up, y_down, y_up]
    cuts = [(0, 0, part), (1, 0, part)]
    for n in range(2, 6):
        cuts += [(n, 0, part), (n, part, bit)]
    offsets = [
        a_at(0), b_at(0),
        a_at(-1), b_at(2), a_at(1), b_at(2) + bit,
        b_at(-1), a_at(2), b_at(1), a_at(2) + bit,
    ]
    za, zb, ya, yb = pieces[2:]
    za, zb = lax.optimization_barrier((za, zb, ya, yb))[:2]
    za, zb = send(za, dc=1), send(zb, dc=1)
    ya, yb = lax.optimization_barrier((ya, yb, za, zb))[:2]
    twins = [send(a, dc=1), send(b, dc=1), za, zb, send(ya, dc=1), send(yb, dc=1)]
    panels = [own, twin] + pieces + twins
    me = lax.axis_index("narrow")
    held = jnp.stack([me, me ^ 1, me ^ 2, me ^ 3]).astype(jnp.int32)
    slot = jnp.sum(
        jnp.where(
            held[:, None] == panel_order[None, :],
            jnp.arange(narrow, dtype=jnp.int32)[None, :],
            0,
        ),
        axis=1,
    ).astype(jnp.int32)
    scalars = jnp.concatenate([held, slot, row_label[0], col_label, sym_map.reshape(-1), jnp.stack(offsets)])
    scalars = scalars.astype(jnp.int32)
    labels = (row_label.shape[1], sym_map.shape[1])
    column = row_energy.reshape(total, 1)
    out = None
    start = 0
    for rows, amp in zip(CHUNKS, amps):
        out, *kept = update_rows(
            amp, panels, tuple(cuts), out, start, total, scalars, labels, column, col_energy
        )
        panels = kept or panels
        start += rows
    return out[None]


def solution(mesh):
    in_specs = (
        P("narrow", None, "wide"),
        P("narrow", None, None),
        P(),
        P("narrow", "wide"),
        P(),
        P(),
        P("narrow", "wide"),
        P(),
    )
    out_specs = P("narrow", "wide", None)
    return jax.shard_map(
        per_device, mesh=mesh, in_specs=in_specs, out_specs=out_specs, check_vma=False
    )
```

```python
import functools
import math
import jax
import jax.numpy as jnp
from jax import lax
from jax.experimental import pallas as pl
from jax.experimental.pallas import tpu as pltpu
from jax.sharding import PartitionSpec as P

AXES = ("wide", "narrow")
CHUNKS = (704, 320)
ANY = pl.BlockSpec(memory_space=pl.ANY)
VMEM = pl.BlockSpec(memory_space=pltpu.VMEM)
HBM = pl.BlockSpec(memory_space=pltpu.HBM)
SMEM = pl.BlockSpec(memory_space=pltpu.SMEM)


def place(i):
    return i // 32, i // 8 % 4, i // 4 % 2 * 2 + i // 2 % 2, i % 2


def shift(devices, dz=0, dy=0, dx=0, dc=0):
    pairs = []
    for i in range(devices):
        z, y, x, c = place(i)
        z, y, x, c = (z + dz) % 4, (y + dy) % 4, (x + dx) % 4, (c + dc) % 2
        pairs.append((i, z * 32 + y * 8 + x // 2 * 4 + x % 2 * 2 + c))
    return pairs


def after(value, *others):
    return lax.optimization_barrier((value, *others))[0]


def cycle_kernel(
    scalar_ref, amp_ref, row_energy_ref, col_energy_ref, *refs, start, slots, labels, cuts
):
    *refs, masked, staged, panels, store_sems, load_sems, keep_sems = refs
    out_ref = refs[-2] if cuts else refs[-1]
    kept = refs[-1] if cuts else refs[0]
    count = max((which for which, _, _ in cuts), default=-1) + 1
    nbc, rows, blk = amp_ref.shape
    unit = math.gcd(math.gcd(start, rows), blk)
    qp = staged.shape[2]
    held, slot, row_label = 0, slots, 2 * slots
    col_label = row_label + labels[0]
    table = col_label + nbc
    offset = table + labels[1] * labels[1]

    def loads(k):
        if not cuts:
            return [pltpu.make_async_copy(kept.at[k], panels.at[k], load_sems.at[k])]
        if k < 2:
            return [pltpu.make_async_copy(refs[k], panels.at[k], load_sems.at[k])]
        out = []
        for n, (which, at, size) in enumerate(cuts):
            to = pl.multiple_of(scalar_ref[offset + n], 128)
            out.append(
                pltpu.make_async_copy(
                    refs[2 + (k - 2) * count + which].at[pl.ds(at, size)],
                    panels.at[k, pl.ds(to, size)],
                    load_sems.at[k],
                )
            )
        return out

    def mask_column(c, carry):
        for i in range(rows // unit):
            row = scalar_ref[row_label + (start + i * unit) // blk]
            kept_block = scalar_ref[table + row * labels[1] + scalar_ref[col_label + c]]
            tile = amp_ref[c, i * unit:(i + 1) * unit, :]
            at = pl.multiple_of(c * blk, blk)
            masked[i * unit:(i + 1) * unit, pl.ds(at, blk)] = tile * kept_block.astype(
                jnp.float32
            ).astype(tile.dtype)
        return carry

    def store(k):
        at = pl.multiple_of(scalar_ref[slot + k] * qp, qp)
        return pltpu.make_async_copy(
            staged.at[k], out_ref.at[pl.ds(start, rows), pl.ds(at, qp)], store_sems.at[k]
        )

    def keep(k):
        return pltpu.make_async_copy(panels.at[k], kept.at[k], keep_sems.at[k])

    for copy in loads(0):
        copy.start()
    lax.fori_loop(0, nbc, mask_column, 0)
    for copy in loads(1):
        copy.start()
    for k in range(slots):
        for copy in loads(k):
            copy.wait()
        if k + 2 < slots:
            for copy in loads(k + 2):
                copy.start()
        if cuts:
            keep(k).start()
        cycle = jnp.dot(masked[...], panels[k], preferred_element_type=jnp.float32)
        energy = row_energy_ref[...] + col_energy_ref[pl.ds(scalar_ref[held + k], 1), :]
        staged[k] = (cycle / energy).astype(staged.dtype)
        store(k).start()
    for k in range(slots):
        store(k).wait()
        if cuts:
            keep(k).wait()


def update_rows(amp, panels, cuts, before, start, total, scalars, labels, row_energy, col_energy):
    nbc, rows, blk = amp.shape
    depth, qp = nbc * blk, panels[0].shape[-1]
    slots = 4
    args = [scalars, amp, row_energy[start:start + rows], col_energy] + panels
    specs = [SMEM] + [VMEM] * 3
    out_shape = [jax.ShapeDtypeStruct((total, slots * qp), jnp.bfloat16)]
    aliases = {}
    if before is None:
        specs += [HBM] * len(panels)
        out_shape.append(jax.ShapeDtypeStruct((slots, depth, qp), amp.dtype))
    else:
        specs += [HBM, ANY]
        aliases = {len(args): 0}
        args.append(before)
        cuts = ()
    return pl.pallas_call(
        functools.partial(cycle_kernel, start=start, slots=slots, labels=labels, cuts=cuts),
        in_specs=specs,
        out_specs=[ANY, HBM][: len(out_shape)],
        scratch_shapes=[
            pltpu.VMEM((rows, depth), amp.dtype),
            pltpu.VMEM((slots, rows, qp), jnp.bfloat16),
            pltpu.VMEM((slots, depth, qp), amp.dtype),
            pltpu.SemaphoreType.DMA((slots,)),
            pltpu.SemaphoreType.DMA((slots,)),
            pltpu.SemaphoreType.DMA((slots,)),
        ],
        out_shape=out_shape,
        input_output_aliases=aliases,
        compiler_params=pltpu.CompilerParams(vmem_limit_bytes=(54 if before is None else 50) * 2**20),
        cost_estimate=pl.CostEstimate(
            flops=2 * rows * depth * qp * slots,
            bytes_accessed=2 * (rows * depth + slots * depth * qp + rows * slots * qp),
            transcendentals=0,
        ),
    )(*args)


def per_device(
    amplitudes, integrals, panel_order, row_label, col_label, sym_map, row_energy, col_energy
):
    wide, narrow = lax.axis_size("wide"), lax.axis_size("narrow")
    total = amplitudes.shape[1] // wide
    blk = amplitudes.shape[2]
    by_target = amplitudes[0].reshape(wide, total, blk)

    def send(value, **way):
        return lax.ppermute(value, AXES, shift(wide * narrow, **way))

    own = integrals[0]
    depth = own.shape[0]
    half, part, bit = depth // 2, depth // 8, depth // 16
    w = lax.axis_index("wide")
    z, y = w // 8, w // 2 % 4

    def a_at(step):
        return (z + 2 * y + 4 + step) % 4 * part

    def b_at(step):
        return half + (2 * z + y + 4 + step) % 4 * part

    a = send(lax.dynamic_slice_in_dim(own, a_at(0), part, 0), dx=1)
    b = send(lax.dynamic_slice_in_dim(own, b_at(0), part, 0), dx=-1)
    twin = send(own, dc=1)
    amps, start = [], 0
    for rows in CHUNKS:
        block = by_target[:, start:start + rows]
        gate = amps[-1:] if amps else [a, b, twin]
        block = after(block, *gate)
        amps.append(lax.all_to_all(block, "wide", split_axis=0, concat_axis=0))
        start += rows
    z_down = send(jnp.concatenate([a, b[:bit]]), dz=1)
    z_up = send(jnp.concatenate([a, b[bit:]]), dz=-1)
    y_down = send(jnp.concatenate([b, a[:bit]]), dy=1)
    y_up = send(jnp.concatenate([b, a[bit:]]), dy=-1)
    pieces = [a, b, z_down, z_up, y_down, y_up]
    cuts = [(0, 0, part), (1, 0, part)]
    for n in range(2, 6):
        cuts += [(n, 0, part), (n, part, bit)]
    offsets = [
        a_at(0), b_at(0),
        a_at(-1), b_at(2), a_at(1), b_at(2) + bit,
        b_at(-1), a_at(2), b_at(1), a_at(2) + bit,
    ]
    za, zb, ya, yb = pieces[2:]
    za, zb = lax.optimization_barrier((za, zb, ya, yb))[:2]
    za, zb = send(za, dc=1), send(zb, dc=1)
    ya, yb = lax.optimization_barrier((ya, yb, za, zb))[:2]
    twins = [send(a, dc=1), send(b, dc=1), za, zb, send(ya, dc=1), send(yb, dc=1)]
    panels = [own, twin] + pieces + twins
    me = lax.axis_index("narrow")
    held = jnp.stack([me, me ^ 1, me ^ 2, me ^ 3]).astype(jnp.int32)
    slot = jnp.sum(
        jnp.where(
            held[:, None] == panel_order[None, :],
            jnp.arange(narrow, dtype=jnp.int32)[None, :],
            0,
        ),
        axis=1,
    ).astype(jnp.int32)
    scalars = jnp.concatenate([held, slot, row_label[0], col_label, sym_map.reshape(-1), jnp.stack(offsets)])
    scalars = scalars.astype(jnp.int32)
    labels = (row_label.shape[1], sym_map.shape[1])
    column = row_energy.reshape(total, 1)
    out = None
    start = 0
    for rows, amp in zip(CHUNKS, amps):
        out, *kept = update_rows(
            amp, panels, tuple(cuts), out, start, total, scalars, labels, column, col_energy
        )
        panels = kept or panels
        start += rows
    return out[None]


def solution(mesh):
    in_specs = (
        P("narrow", None, "wide"),
        P("narrow", None, None),
        P(),
        P("narrow", "wide"),
        P(),
        P(),
        P("narrow", "wide"),
        P(),
    )
    out_specs = P("narrow", "wide", None)
    return jax.shard_map(
        per_device, mesh=mesh, in_specs=in_specs, out_specs=out_specs, check_vma=False
    )
```
